32 devices in a mesh: groups: 2 (over y), blk: 8 (over z, x), mp: 2 (over core).
Axes of the slice: x: 2, y: 2, z: 4, core: 2. Of those that a mesh axis runs over, the one named last changes fastest.
Arguments:
- probe_vectors: bfloat16 [12, 8, 32, 3584], P('groups', 'blk', None, 'mp'), parts along dimension 0, may hold values from -12 to 12
- unsettled_lookups: bfloat16 [12, 8, 32, 512], P('groups', 'blk', None, 'mp'), parts along dimension 0, may hold values from -6 to 6
- unsettled_payloads: bfloat16 [12, 8, 32, 512], P('groups', 'blk', None, 'mp'), parts along dimension 0, may hold values from -6 to 6
- uncover_ordering: int32 [12, 8, 32], P('groups', 'blk'), parts along dimension 0, may hold values from 0 to 31, each once within a row
- rounds_finished: int32 [12, 8], P('groups', 'blk'), parts along dimension 0, may hold values from 0 to 7
- random_entry_choice: int32 [12, 8, 32], P('groups', 'blk'), parts along dimension 0, may hold values from 0 to 63
- noise_token_keys: bfloat16 [64, 512], P(None, 'mp'), may hold values from -6 to 6
- noise_token_values: bfloat16 [64, 512], P(None, 'mp'), may hold values from -6 to 6
- prefix_key_cache: bfloat16 [2, 8, 32, 512], P('groups', 'blk', None, 'mp'), parts along dimension 0, may hold values from -6 to 6
- prefix_value_cache: bfloat16 [2, 8, 32, 512], P('groups', 'blk', None, 'mp'), parts along dimension 0, may hold values from -6 to 6
- completed_keys: bfloat16 [16, 32, 512], P(('groups', 'blk'), None, 'mp'), parts along dimension 0, may hold values from -6 to 6
- completed_values: bfloat16 [16, 32, 512], P(('groups', 'blk'), None, 'mp'), parts along dimension 0, may hold values from -6 to 6
- committing_index: int32 [2], P('groups'), parts along dimension 0, may hold values from 0 to 7, as said below
Outputs:
- attended: bfloat16 [12, 8, 32, 3584], P('groups', 'blk', None, 'mp'), parts along dimension 0
The draws below stay inside these ranges and needn't reach their ends.
There are 2 independent parts, one for each index of `groups`. The reference program is written for one: setup_inputs(seed, part) draws one part's arguments, and reference() takes and returns one part's arrays. A program takes and returns all parts, laid end to end along the dimension named above; an argument that names none is the same for every part. Nothing has to cross between parts.
Inputs may be any that keep to these rules, and one draw needn't show every extreme that they name: `committing_index`: an index of blk; in every odd part it is the last index, 7.
All inputs are finite; a program needn't handle non-finite values.
Results may differ from the reference program's by a relative error of at most 0.005.
Values may be sent and summed in bfloat16 or wider, within the bound.
A program may use at most 128 MiB of HBM per device.

```python
import jax
import jax.numpy as jnp
from jax import lax

QUERY_GROUPS = 28
MEMORY_GROUPS = 4
FEATURE_DIM = 128
SPAN_LENGTH = 32
DENOISE_ROUNDS = 8
RANDOM_ROWS = 64
OPEN_ON_LANE = 6
CB = 1
UNMASK = 4
OPEN_COUNT = 48
PREFIX = 256
N_BLK = 8


def draw_committing_index(key, part):
    halfway = jax.random.randint(jax.random.fold_in(key, 11), (1,), 0, N_BLK // 2)
    parity = jnp.asarray(part, jnp.int32) % 2
    last_index = jnp.full((1,), N_BLK - 1, jnp.int32)
    return jnp.where(parity == 1, last_index, 2 * halfway).astype(jnp.int32)


def draw_prefix_key_cache(key, part):
    starting_point = jnp.clip(jax.random.normal(jax.random.fold_in(key, 1), (CB, N_BLK, SPAN_LENGTH, MEMORY_GROUPS * FEATURE_DIM), jnp.float32), -6.0, 6.0)
    return starting_point.astype(jnp.bfloat16)


def draw_probe_vectors(key, part):
    starting_point = jnp.clip(2.0 * jax.random.normal(jax.random.fold_in(key, 4), (OPEN_ON_LANE, N_BLK, SPAN_LENGTH, QUERY_GROUPS * FEATURE_DIM), jnp.float32), -12.0, 12.0)
    return starting_point.astype(jnp.bfloat16)


def touch_ends(values, rng, smallest, high):
    longest = values.shape.index(max(values.shape))
    spots = []
    for shift in (0, 1):
        where = [jax.random.randint(jax.random.fold_in(rng, axis), (), 0, length) for axis, length in enumerate(values.shape)]
        where[longest] = (where[longest] + shift) % values.shape[longest]
        spots.append(tuple(where))
    return values.at[spots[0]].set(smallest).at[spots[1]].set(high)


def level_of(rng, shape, pieces, smallest, high):
    factor_of, own = 1.0, jax.random.fold_in(rng, 6)
    for position, shards_of in pieces:
        heights = jnp.exp(jax.random.uniform(jax.random.fold_in(own, position), (shards_of,), jnp.float32, smallest / len(pieces), high / len(pieces)))
        factor_of = factor_of * jnp.repeat(heights, shape[position] // shards_of).reshape([-1 if axis == position else 1 for axis in range(len(shape))])
    return factor_of


def bell_draw(own_key, dims, spread, reach, cuts=(), kind=jnp.bfloat16):
    array = spread * jax.random.normal(own_key, dims, jnp.float32)
    if cuts:
        array = array * level_of(own_key, dims, cuts, -0.22, 0.18)
    return jnp.clip(array, -reach, reach).astype(kind)


def setup_inputs(seed: int = 0, part: int = 0) -> dict:
    seeds = jax.random.split(jax.random.key(seed), 14)
    own_keys = jax.random.split(jax.random.fold_in(seeds[13], part), 14)
    probe_vectors = draw_probe_vectors(jax.random.fold_in(jax.random.fold_in(seeds[13], part), 71), part)
    unsettled_lookups = bell_draw(own_keys[1], (OPEN_ON_LANE, N_BLK, SPAN_LENGTH, MEMORY_GROUPS * FEATURE_DIM), 1.0, 6.0, ((1, 8), (3, 2)))
    unsettled_payloads = bell_draw(own_keys[2], (OPEN_ON_LANE, N_BLK, SPAN_LENGTH, MEMORY_GROUPS * FEATURE_DIM), 1.0, 6.0, ((1, 8), (3, 2)))
    uncover_ordering = jax.vmap(lambda own: jax.random.permutation(own, SPAN_LENGTH))(jax.random.split(own_keys[3], OPEN_ON_LANE * N_BLK)).reshape((OPEN_ON_LANE, N_BLK, SPAN_LENGTH)).astype(jnp.int32)
    rounds_finished = touch_ends(jax.random.randint(own_keys[4], (OPEN_ON_LANE, N_BLK), 0, DENOISE_ROUNDS), jax.random.fold_in(own_keys[4], 1), 0, DENOISE_ROUNDS - 1).astype(jnp.int32)
    random_entry_choice = touch_ends(jax.random.randint(own_keys[5], (OPEN_ON_LANE, N_BLK, SPAN_LENGTH), 0, RANDOM_ROWS), jax.random.fold_in(own_keys[5], 1), 0, RANDOM_ROWS - 1).astype(jnp.int32)
    noise_token_keys = bell_draw(seeds[6], (RANDOM_ROWS, MEMORY_GROUPS * FEATURE_DIM), 1.0, 6.0, ((1, 2),))
    noise_token_values = bell_draw(seeds[7], (RANDOM_ROWS, MEMORY_GROUPS * FEATURE_DIM), 1.0, 6.0, ((1, 2),))
    prefix_key_cache = draw_prefix_key_cache(jax.random.fold_in(jax.random.fold_in(seeds[13], part), 71), part)
    prefix_value_cache = bell_draw(own_keys[9], (CB, N_BLK, SPAN_LENGTH, MEMORY_GROUPS * FEATURE_DIM), 1.0, 6.0, ((1, 8), (3, 2)))
    completed_keys = bell_draw(own_keys[10], (N_BLK, SPAN_LENGTH, MEMORY_GROUPS * FEATURE_DIM), 1.0, 6.0, ((0, 8), (2, 2)))
    completed_values = bell_draw(own_keys[11], (N_BLK, SPAN_LENGTH, MEMORY_GROUPS * FEATURE_DIM), 1.0, 6.0, ((0, 8), (2, 2)))
    committing_index = draw_committing_index(jax.random.fold_in(jax.random.fold_in(seeds[13], part), 71), part)
    return dict(probe_vectors=probe_vectors, unsettled_lookups=unsettled_lookups, unsettled_payloads=unsettled_payloads, uncover_ordering=uncover_ordering, rounds_finished=rounds_finished, random_entry_choice=random_entry_choice, noise_token_keys=noise_token_keys, noise_token_values=noise_token_values, prefix_key_cache=prefix_key_cache, prefix_value_cache=prefix_value_cache, completed_keys=completed_keys, completed_values=completed_values, committing_index=committing_index)


def reference(probe_vectors, unsettled_lookups, unsettled_payloads, uncover_ordering, rounds_finished, random_entry_choice, noise_token_keys, noise_token_values, prefix_key_cache, prefix_value_cache, completed_keys, completed_values, committing_index):
    concealed_flags = uncover_ordering >= UNMASK * rounds_finished[:, :, None]
    onehot = (random_entry_choice[..., None] == jnp.arange(RANDOM_ROWS, dtype=jnp.int32)).astype(jnp.float32)
    blended_lookups = jnp.einsum('sjtn,nc->sjtc', onehot, noise_token_keys.astype(jnp.float32)).astype(jnp.bfloat16)
    blended_payloads = jnp.einsum('sjtn,nc->sjtc', onehot, noise_token_values.astype(jnp.float32)).astype(jnp.bfloat16)
    own_span_lookups = jnp.where(concealed_flags[..., None], blended_lookups, unsettled_lookups).reshape(OPEN_COUNT, SPAN_LENGTH, MEMORY_GROUPS * FEATURE_DIM)
    own_span_payloads = jnp.where(concealed_flags[..., None], blended_payloads, unsettled_payloads).reshape(OPEN_COUNT, SPAN_LENGTH, MEMORY_GROUPS * FEATURE_DIM)
    prev_keys = jnp.roll(own_span_lookups, 1, axis=0)
    prev_values = jnp.roll(own_span_payloads, 1, axis=0)
    owner = committing_index[0].astype(jnp.int32)
    commit_keys = lax.dynamic_index_in_dim(completed_keys, owner, 0, keepdims=False)
    commit_values = lax.dynamic_index_in_dim(completed_values, owner, 0, keepdims=False)
    prefix_keys = prefix_key_cache.reshape(PREFIX, MEMORY_GROUPS * FEATURE_DIM)
    prefix_values = prefix_value_cache.reshape(PREFIX, MEMORY_GROUPS * FEATURE_DIM)
    group = QUERY_GROUPS // MEMORY_GROUPS
    scale = FEATURE_DIM ** -0.5
    flattened_probes = probe_vectors.reshape(OPEN_COUNT, SPAN_LENGTH, QUERY_GROUPS * FEATURE_DIM)

    def one_block(items):
        query, pk, pv, ok, ov = items
        keys = jnp.concatenate([prefix_keys, commit_keys, pk, ok], axis=0).reshape(-1, MEMORY_GROUPS, FEATURE_DIM).astype(jnp.float32)
        values = jnp.concatenate([prefix_values, commit_values, pv, ov], axis=0).reshape(-1, MEMORY_GROUPS, FEATURE_DIM).astype(jnp.float32)
        qf = query.reshape(SPAN_LENGTH, MEMORY_GROUPS, group, FEATURE_DIM).astype(jnp.float32)
        score = jnp.einsum('tgrd,lgd->grtl', qf, keys) * scale
        top = jnp.max(score, axis=-1, keepdims=True)
        weight = jnp.exp(score - top)
        total = jnp.sum(weight, axis=-1)
        rounded = weight.astype(jnp.bfloat16).astype(jnp.float32)
        summed = jnp.einsum('grtl,lgd->tgrd', rounded, values)
        attended_output = summed / jnp.transpose(total, (2, 0, 1))[..., None]
        return attended_output.reshape(SPAN_LENGTH, QUERY_GROUPS * FEATURE_DIM)

    attended_output = lax.map(one_block, (flattened_probes, prev_keys, prev_values, own_span_lookups, own_span_payloads))
    attended_output = attended_output.reshape(OPEN_ON_LANE, N_BLK, SPAN_LENGTH, QUERY_GROUPS * FEATURE_DIM)
    return jnp.where(concealed_flags[..., None], attended_output, 0.0).astype(jnp.bfloat16)
```

```python
import functools
import math

import jax
import jax.numpy as jnp
from jax import lax
from jax.experimental import pallas as pl
from jax.experimental.pallas import tpu as pltpu
from jax.sharding import PartitionSpec as P

QUERY_GROUPS = 28
MEMORY_GROUPS = 4
FEATURE_DIM = 128
UNMASK = 4
GROUP = QUERY_GROUPS // MEMORY_GROUPS
CHUNK = 8
MESH = pl.DeviceIdType.MESH
F32 = jnp.float32
BF16 = jnp.bfloat16


def over_rows(a, b):
    return lax.dot_general(a, b, (((0,), (0,)), ((), ())), preferred_element_type=F32)


def over_lanes(a, b):
    return lax.dot_general(a, b, (((1,), (1,)), ((), ())), preferred_element_type=F32)


def kernel(
    n,
    order_hbm,
    rounds_hbm,
    choice_hbm,
    index_hbm,
    noise_k_hbm,
    noise_v_hbm,
    q_hbm,
    uk_hbm,
    uv_hbm,
    pk_hbm,
    pv_hbm,
    ck_hbm,
    cv_hbm,
    out_hbm,
    order_ref,
    rounds_ref,
    choice_ref,
    index_ref,
    table,
    q,
    uk,
    uv,
    own,
    prev,
    gath,
    maskf,
    res,
    local_sem,
    out_sem,
    gsend,
    grecv,
    ssend,
    srecv,
):
    slots, block, _ = own.shape
    width = noise_k_hbm.shape[1]
    heads = width // FEATURE_DIM
    me = lax.axis_index("blk")
    barrier = pltpu.get_barrier_semaphore()

    @pl.loop(1, n)
    def _(d):
        pl.semaphore_signal(
            barrier, inc=1, device_id={"blk": lax.rem(me + d, n)}, device_id_type=MESH
        )

    loads = [
        pltpu.make_async_copy(src, dst, local_sem.at[i])
        for i, (src, dst) in enumerate(
            (
                (order_hbm, order_ref),
                (rounds_hbm, rounds_ref),
                (choice_hbm, choice_ref),
                (noise_k_hbm, table.at[:, pl.ds(0, width)]),
                (noise_v_hbm, table.at[:, pl.ds(width, width)]),
                (uk_hbm.at[:, 0], uk),
                (uv_hbm.at[:, 0], uv),
                (pk_hbm.at[0, 0], gath.at[me, pl.ds(0, block), pl.ds(0, width)]),
                (pv_hbm.at[0, 0], gath.at[me, pl.ds(0, block), pl.ds(width, width)]),
                (ck_hbm.at[0], gath.at[me, pl.ds(block, block), pl.ds(0, width)]),
                (cv_hbm.at[0], gath.at[me, pl.ds(block, block), pl.ds(width, width)]),
                (index_hbm, index_ref),
                (q_hbm.at[:, 0], q),
            )
        )
    ]
    for load in loads:
        load.start()
    for load in loads[:7]:
        load.wait()

    entries = table.shape[0]
    row_n = lax.broadcasted_iota(jnp.int32, (entries, block), 0)
    row_b = lax.broadcasted_iota(jnp.int32, (block, block), 0)
    col_b = lax.broadcasted_iota(jnp.int32, (block, block), 1)
    ones_n = jnp.ones((entries, FEATURE_DIM), BF16)
    for s in range(slots):
        hidden = order_ref[s] >= UNMASK * rounds_ref[s]
        noise = jnp.where((row_n == choice_ref[s]) & hidden, 1.0, 0.0).astype(BF16)
        keep = jnp.where((row_b == col_b) & jnp.logical_not(hidden), 1.0, 0.0).astype(BF16)
        shown = jnp.concatenate([uk[s], uv[s]], axis=1)
        own[s] = over_rows(
            jnp.concatenate([noise, keep], axis=0), jnp.concatenate([table[...], shown], axis=0)
        ).astype(BF16)
        maskf[s] = over_rows(noise, ones_n)

    for load in loads[7:11]:
        load.wait()
    pl.semaphore_wait(barrier, n - 1)

    after = lax.rem(me + 1, n)
    wrap = me // (n - 1)

    def shift(s):
        to = lax.rem(s + wrap, slots)
        return pltpu.make_async_remote_copy(
            src_ref=own.at[s],
            dst_ref=prev.at[to],
            send_sem=ssend.at[s],
            recv_sem=srecv.at[to],
            device_id={"blk": after},
            device_id_type=MESH,
        )

    def spread(d):
        return pltpu.make_async_remote_copy(
            src_ref=gath.at[me],
            dst_ref=gath.at[me],
            send_sem=gsend.at[d],
            recv_sem=grecv.at[me],
            device_id={"blk": lax.rem(me + d, n)},
            device_id_type=MESH,
        )

    def spread_in(d):
        j = lax.rem(me + d, n)
        return pltpu.make_async_remote_copy(
            src_ref=gath.at[j],
            dst_ref=gath.at[j],
            send_sem=gsend.at[d],
            recv_sem=grecv.at[j],
            device_id={"blk": j},
            device_id_type=MESH,
        )

    def shift_in(s):
        return pltpu.make_async_remote_copy(
            src_ref=own.at[s],
            dst_ref=prev.at[s],
            send_sem=ssend.at[s],
            recv_sem=srecv.at[s],
            device_id={"blk": after},
            device_id_type=MESH,
        )

    @pl.loop(1, n)
    def _(d):
        spread(d).start()

    for s in range(slots):
        shift(s).start()

    loads[11].wait()
    loads[12].wait()

    @pl.loop(1, n)
    def _(d):
        spread_in(d).wait_recv()

    factor = FEATURE_DIM**-0.5 * math.log2(math.e)
    owner = index_ref[0]
    commit = gath[owner, block:, :]

    def lanes(g):
        return slice(g * FEATURE_DIM, (g + 1) * FEATURE_DIM)

    def with_ones(v):
        return jnp.concatenate([v, jnp.ones(v.shape, BF16)], axis=1)

    def shared(c, col):
        part = gath[pl.ds(c * CHUNK, CHUNK), 0:block, col]
        return part.reshape(CHUNK * block, FEATURE_DIM)

    @pl.loop(0, slots)
    def _(s):
        shift_in(s).wait_recv()
        for g in range(heads):
            first = g * GROUP
            qs = jnp.concatenate([q[s, :, lanes(first + r)] for r in range(GROUP)], axis=0)
            kc, vc = lanes(g), lanes(heads + g)
            k2 = jnp.concatenate([prev[s, :, kc], own[s, :, kc], commit[:, kc]], axis=0)
            v2 = jnp.concatenate([prev[s, :, vc], own[s, :, vc], commit[:, vc]], axis=0)
            s1 = over_lanes(qs, shared(0, kc))
            s2 = over_lanes(qs, k2)
            top = jnp.maximum(
                jnp.max(s1, axis=1, keepdims=True), jnp.max(s2, axis=1, keepdims=True)
            )
            p1 = jnp.exp2((s1 - top) * factor).astype(BF16)
            p2 = jnp.exp2((s2 - top) * factor).astype(BF16)
            acc = jnp.dot(p1, with_ones(shared(0, vc)), preferred_element_type=F32)
            acc = acc + jnp.dot(p2, with_ones(v2), preferred_element_type=F32)
            if n > CHUNK:

                def more(c, state):
                    top, acc = state
                    s1 = over_lanes(qs, shared(c, kc))
                    new = jnp.maximum(top, jnp.max(s1, axis=1, keepdims=True))
                    p1 = jnp.exp2((s1 - new) * factor).astype(BF16)
                    part = jnp.dot(p1, with_ones(shared(c, vc)), preferred_element_type=F32)
                    return new, acc * jnp.exp2((top - new) * factor) + part

                top, acc = lax.fori_loop(1, n // CHUNK, more, (top, acc))
            o = acc[:, :FEATURE_DIM] / acc[:, FEATURE_DIM:]
            mask = maskf[s]
            for r in range(GROUP):
                part = o[r * block : (r + 1) * block] * mask
                res[s, :, lanes(first + r)] = part.astype(BF16)
        pltpu.make_async_copy(res.at[s], out_hbm.at[s, 0], out_sem.at[s]).start()

    @pl.loop(1, n)
    def _(d):
        spread(d).wait_send()

    for s in range(slots):
        shift_in(s).wait_send()
        pltpu.make_async_copy(res.at[s], out_hbm.at[s, 0], out_sem.at[s]).wait()


def on_device(
    n,
    probe_vectors,
    unsettled_lookups,
    unsettled_payloads,
    uncover_ordering,
    rounds_finished,
    random_entry_choice,
    noise_token_keys,
    noise_token_values,
    prefix_key_cache,
    prefix_value_cache,
    completed_keys,
    completed_values,
    committing_index,
):
    slots, _, block, columns = probe_vectors.shape
    width = noise_token_keys.shape[1]
    anywhere = pl.BlockSpec(memory_space=pl.ANY)
    return pl.pallas_call(
        functools.partial(kernel, n),
        out_shape=jax.ShapeDtypeStruct(probe_vectors.shape, BF16),
        in_specs=[pl.BlockSpec(memory_space=pltpu.HBM)] * 13,
        out_specs=anywhere,
        scratch_shapes=[
            pltpu.VMEM(uncover_ordering.shape, jnp.int32),
            pltpu.SMEM((slots,), jnp.int32),
            pltpu.VMEM(random_entry_choice.shape, jnp.int32),
            pltpu.SMEM((1,), jnp.int32),
            pltpu.VMEM((noise_token_keys.shape[0], 2 * width), BF16),
            pltpu.VMEM((slots, block, columns), BF16),
            pltpu.VMEM((slots, block, width), BF16),
            pltpu.VMEM((slots, block, width), BF16),
            pltpu.VMEM((slots, block, 2 * width), BF16),
            pltpu.VMEM((slots, block, 2 * width), BF16),
            pltpu.VMEM((n, 2 * block, 2 * width), BF16),
            pltpu.VMEM((slots, block, FEATURE_DIM), F32),
            pltpu.VMEM((slots, block, columns), BF16),
            pltpu.SemaphoreType.DMA((13,)),
            pltpu.SemaphoreType.DMA((slots,)),
            pltpu.SemaphoreType.DMA((n,)),
            pltpu.SemaphoreType.DMA((n,)),
            pltpu.SemaphoreType.DMA((slots,)),
            pltpu.SemaphoreType.DMA((slots,)),
        ],
        compiler_params=pltpu.CompilerParams(
            collective_id=0, has_side_effects=True, vmem_limit_bytes=60 * 2**20
        ),
    )(
        uncover_ordering,
        rounds_finished.reshape(slots),
        random_entry_choice,
        committing_index,
        noise_token_keys,
        noise_token_values,
        probe_vectors,
        unsettled_lookups,
        unsettled_payloads,
        prefix_key_cache,
        prefix_value_cache,
        completed_keys,
        completed_values,
    )


def solution(mesh):
    wide = P("groups", "blk", None, "mp")
    placed = (
        wide,
        wide,
        wide,
        P("groups", "blk", None),
        P("groups", "blk"),
        P("groups", "blk", None),
        P(None, "mp"),
        P(None, "mp"),
        wide,
        wide,
        P(("groups", "blk"), None, "mp"),
        P(("groups", "blk"), None, "mp"),
        P("groups"),
    )
    return jax.shard_map(
        functools.partial(on_device, mesh.shape["blk"]),
        mesh=mesh,
        in_specs=placed,
        out_specs=wide,
        check_vma=False,
    )
```

```python
import functools
import math

import jax
import jax.numpy as jnp
from jax import lax
from jax.experimental import pallas as pl
from jax.experimental.pallas import tpu as pltpu
from jax.sharding import PartitionSpec as P

QUERY_GROUPS = 28
MEMORY_GROUPS = 4
FEATURE_DIM = 128
UNMASK = 4
GROUP = QUERY_GROUPS // MEMORY_GROUPS
HALF = 4
MESH = pl.DeviceIdType.MESH
F32 = jnp.float32
BF16 = jnp.bfloat16


def over_rows(a, b):
    return lax.dot_general(a, b, (((0,), (0,)), ((), ())), preferred_element_type=F32)


def over_lanes(a, b):
    return lax.dot_general(a, b, (((1,), (1,)), ((), ())), preferred_element_type=F32)


def kernel(
    n,
    order_hbm,
    rounds_hbm,
    choice_hbm,
    index_hbm,
    noise_k_hbm,
    noise_v_hbm,
    q_hbm,
    uk_hbm,
    uv_hbm,
    pk_hbm,
    pv_hbm,
    ck_hbm,
    cv_hbm,
    out,
    order_ref,
    rounds_ref,
    choice_ref,
    index_ref,
    table,
    q,
    uk,
    uv,
    own,
    prev,
    col,
    oth,
    com,
    maskf,
    local_sem,
    gsend,
    grecv,
    fsend,
    frecv,
    ssend,
    srecv,
):
    slots, block, _ = own.shape
    width = noise_k_hbm.shape[1]
    heads = width // FEATURE_DIM
    me = lax.axis_index("blk")
    barrier = pltpu.get_barrier_semaphore()

    rows = n // 2
    row, par = me // 2, lax.rem(me, 2)
    partner = me + 1 - 2 * par

    def greet(d):
        pl.semaphore_signal(
            barrier, inc=1, device_id={"blk": lax.rem(me + d, n)}, device_id_type=MESH
        )

    greet(1)
    greet(n - 1)
    pl.loop(1, rows)(lambda d: greet(2 * d))

    loads = [
        pltpu.make_async_copy(src, dst, local_sem.at[i])
        for i, (src, dst) in enumerate(
            (
                (order_hbm, order_ref),
                (rounds_hbm, rounds_ref),
                (choice_hbm, choice_ref),
                (noise_k_hbm, table.at[:, pl.ds(0, width)]),
                (noise_v_hbm, table.at[:, pl.ds(width, width)]),
                (uk_hbm.at[:, 0], uk),
                (uv_hbm.at[:, 0], uv),
                (pk_hbm.at[0, 0], col.at[row, pl.ds(0, block), pl.ds(0, width)]),
                (pv_hbm.at[0, 0], col.at[row, pl.ds(0, block), pl.ds(width, width)]),
                (ck_hbm.at[0], col.at[row, pl.ds(block, block), pl.ds(0, width)]),
                (cv_hbm.at[0], col.at[row, pl.ds(block, block), pl.ds(width, width)]),
                (index_hbm, index_ref),
                (q_hbm.at[:, 0], q),
            )
        )
    ]
    for load in loads:
        load.start()
    for load in loads[:7]:
        load.wait()

    entries = table.shape[0]
    row_n = lax.broadcasted_iota(jnp.int32, (entries, block), 0)
    row_b = lax.broadcasted_iota(jnp.int32, (block, block), 0)
    col_b = lax.broadcasted_iota(jnp.int32, (block, block), 1)
    ones_n = jnp.ones((entries, FEATURE_DIM), BF16)
    for s in range(slots):
        hidden = order_ref[s] >= UNMASK * rounds_ref[s]
        noise = jnp.where((row_n == choice_ref[s]) & hidden, 1.0, 0.0).astype(BF16)
        keep = jnp.where((row_b == col_b) & jnp.logical_not(hidden), 1.0, 0.0).astype(BF16)
        shown = jnp.concatenate([uk[s], uv[s]], axis=1)
        own[s] = over_rows(
            jnp.concatenate([noise, keep], axis=0), jnp.concatenate([table[...], shown], axis=0)
        ).astype(BF16)
        maskf[s] = over_rows(noise, ones_n)

    for load in loads[7:11]:
        load.wait()
    pl.semaphore_wait(barrier, rows + 1)

    after = lax.rem(me + 1, n)
    wrap = me // (n - 1)

    def shift(s):
        to = lax.rem(s + wrap, slots)
        return pltpu.make_async_remote_copy(
            src_ref=own.at[s],
            dst_ref=prev.at[to],
            send_sem=ssend.at[s],
            recv_sem=srecv.at[to],
            device_id={"blk": after},
            device_id_type=MESH,
        )

    def spread(d):
        return pltpu.make_async_remote_copy(
            src_ref=col.at[row],
            dst_ref=col.at[row],
            send_sem=gsend.at[d],
            recv_sem=grecv.at[row],
            device_id={"blk": 2 * lax.rem(row + d, rows) + par},
            device_id_type=MESH,
        )

    def spread_in(j):
        return pltpu.make_async_remote_copy(
            src_ref=col.at[j],
            dst_ref=col.at[j],
            send_sem=gsend.at[0],
            recv_sem=grecv.at[j],
            device_id={"blk": partner},
            device_id_type=MESH,
        )

    def relay(j):
        return pltpu.make_async_remote_copy(
            src_ref=col.at[j, pl.ds(0, block)],
            dst_ref=oth.at[j],
            send_sem=fsend.at[j],
            recv_sem=frecv.at[j],
            device_id={"blk": partner},
            device_id_type=MESH,
        )

    def chosen(mine):
        return pltpu.make_async_remote_copy(
            src_ref=com.at[mine],
            dst_ref=com.at[mine],
            send_sem=fsend.at[rows],
            recv_sem=frecv.at[rows],
            device_id={"blk": partner},
            device_id_type=MESH,
        )

    def shift_in(s):
        return pltpu.make_async_remote_copy(
            src_ref=own.at[s],
            dst_ref=prev.at[s],
            send_sem=ssend.at[s],
            recv_sem=srecv.at[s],
            device_id={"blk": after},
            device_id_type=MESH,
        )

    @pl.loop(1, rows)
    def _(d):
        spread(d).start()

    relay(row).start()

    for s in range(slots):
        shift(s).start()

    loads[11].wait()
    owner = index_ref[0]

    @pl.loop(1, rows)
    def _(d):
        j = lax.rem(row + d, rows)
        spread_in(j).wait_recv()
        relay(j).start()

    com[par] = col[owner // 2, block:, :]
    chosen(par).start()
    loads[12].wait()

    @pl.loop(0, rows)
    def _(j):
        relay(j).wait_recv()

    chosen(1 - par).wait_recv()

    factor = FEATURE_DIM**-0.5 * math.log2(math.e)
    commit = com[lax.rem(owner, 2)]

    def lanes(g):
        return slice(g * FEATURE_DIM, (g + 1) * FEATURE_DIM)

    def with_ones(v):
        return jnp.concatenate([v, jnp.ones(v.shape, BF16)], axis=1)

    def shared(c, where):
        near = col[pl.ds(c * HALF, HALF), 0:block, where].reshape(HALF * block, FEATURE_DIM)
        far = oth[pl.ds(c * HALF, HALF), :, where].reshape(HALF * block, FEATURE_DIM)
        return jnp.concatenate([near, far], axis=0)

    @pl.loop(0, slots, unroll=2)
    def _(s):
        shift_in(s).wait_recv()
        for g in range(heads):
            first = g * GROUP
            qs = jnp.concatenate([q[s, :, lanes(first + r)] for r in range(GROUP)], axis=0)
            kc, vc = lanes(g), lanes(heads + g)
            k2 = jnp.concatenate([prev[s, :, kc], own[s, :, kc], commit[:, kc]], axis=0)
            v2 = jnp.concatenate([prev[s, :, vc], own[s, :, vc], commit[:, vc]], axis=0)
            s1 = over_lanes(qs, shared(0, kc))
            s2 = over_lanes(qs, k2)
            top = jnp.maximum(
                jnp.max(s1, axis=1, keepdims=True), jnp.max(s2, axis=1, keepdims=True)
            )
            p1 = jnp.exp2((s1 - top) * factor).astype(BF16)
            p2 = jnp.exp2((s2 - top) * factor).astype(BF16)
            acc = jnp.dot(p1, with_ones(shared(0, vc)), preferred_element_type=F32)
            acc = acc + jnp.dot(p2, with_ones(v2), preferred_element_type=F32)
            if rows > HALF:

                def more(c, state):
                    top, acc = state
                    s1 = over_lanes(qs, shared(c, kc))
                    new = jnp.maximum(top, jnp.max(s1, axis=1, keepdims=True))
                    p1 = jnp.exp2((s1 - new) * factor).astype(BF16)
                    part = jnp.dot(p1, with_ones(shared(c, vc)), preferred_element_type=F32)
                    return new, acc * jnp.exp2((top - new) * factor) + part

                top, acc = lax.fori_loop(1, rows // HALF, more, (top, acc))
            o = acc[:, :FEATURE_DIM] / acc[:, FEATURE_DIM:]
            mask = maskf[s]
            for r in range(GROUP):
                part = o[r * block : (r + 1) * block] * mask
                out[s, 0, :, lanes(first + r)] = part.astype(BF16)

    @pl.loop(1, rows)
    def _(d):
        spread(d).wait_send()

    @pl.loop(0, rows)
    def _(j):
        relay(j).wait_send()

    chosen(par).wait_send()

    for s in range(slots):
        shift_in(s).wait_send()


def on_device(
    n,
    probe_vectors,
    unsettled_lookups,
    unsettled_payloads,
    uncover_ordering,
    rounds_finished,
    random_entry_choice,
    noise_token_keys,
    noise_token_values,
    prefix_key_cache,
    prefix_value_cache,
    completed_keys,
    completed_values,
    committing_index,
):
    slots, _, block, columns = probe_vectors.shape
    width = noise_token_keys.shape[1]
    anywhere = pl.BlockSpec(memory_space=pl.ANY)
    return pl.pallas_call(
        functools.partial(kernel, n),
        out_shape=pltpu.VMEM(probe_vectors.shape, BF16),
        in_specs=[pl.BlockSpec(memory_space=pltpu.HBM)] * 13,
        out_specs=pl.BlockSpec(memory_space=pltpu.VMEM),
        scratch_shapes=[
            pltpu.VMEM(uncover_ordering.shape, jnp.int32),
            pltpu.SMEM((slots,), jnp.int32),
            pltpu.VMEM(random_entry_choice.shape, jnp.int32),
            pltpu.SMEM((1,), jnp.int32),
            pltpu.VMEM((noise_token_keys.shape[0], 2 * width), BF16),
            pltpu.VMEM((slots, block, columns), BF16),
            pltpu.VMEM((slots, block, width), BF16),
            pltpu.VMEM((slots, block, width), BF16),
            pltpu.VMEM((slots, block, 2 * width), BF16),
            pltpu.VMEM((slots, block, 2 * width), BF16),
            pltpu.VMEM((n // 2, 2 * block, 2 * width), BF16),
            pltpu.VMEM((n // 2, block, 2 * width), BF16),
            pltpu.VMEM((2, block, 2 * width), BF16),
            pltpu.VMEM((slots, block, FEATURE_DIM), F32),
            pltpu.SemaphoreType.DMA((13,)),
            pltpu.SemaphoreType.DMA((n // 2,)),
            pltpu.SemaphoreType.DMA((n // 2,)),
            pltpu.SemaphoreType.DMA((n // 2 + 1,)),
            pltpu.SemaphoreType.DMA((n // 2 + 1,)),
            pltpu.SemaphoreType.DMA((slots,)),
            pltpu.SemaphoreType.DMA((slots,)),
        ],
        compiler_params=pltpu.CompilerParams(
            collective_id=0, has_side_effects=True, vmem_limit_bytes=60 * 2**20
        ),
    )(
        uncover_ordering,
        rounds_finished.reshape(slots),
        random_entry_choice,
        committing_index,
        noise_token_keys,
        noise_token_values,
        probe_vectors,
        unsettled_lookups,
        unsettled_payloads,
        prefix_key_cache,
        prefix_value_cache,
        completed_keys,
        completed_values,
    )


def solution(mesh):
    wide = P("groups", "blk", None, "mp")
    placed = (
        wide,
        wide,
        wide,
        P("groups", "blk", None),
        P("groups", "blk"),
        P("groups", "blk", None),
        P(None, "mp"),
        P(None, "mp"),
        wide,
        wide,
        P(("groups", "blk"), None, "mp"),
        P(("groups", "blk"), None, "mp"),
        P("groups"),
    )
    return jax.shard_map(
        functools.partial(on_device, mesh.shape["blk"]),
        mesh=mesh,
        in_specs=placed,
        out_specs=wide,
        check_vma=False,
    )
```

```python
import functools
import math

import jax
import jax.numpy as jnp
from jax import lax
from jax.experimental import pallas as pl
from jax.experimental.pallas import tpu as pltpu
from jax.sharding import PartitionSpec as P

QUERY_GROUPS = 28
MEMORY_GROUPS = 4
FEATURE_DIM = 128
UNMASK = 4
GROUP = QUERY_GROUPS // MEMORY_GROUPS
HALF = 4
MESH = pl.DeviceIdType.MESH
F32 = jnp.float32
BF16 = jnp.bfloat16


def over_rows(a, b):
    return lax.dot_general(a, b, (((0,), (0,)), ((), ())), preferred_element_type=F32)


def over_lanes(a, b):
    return lax.dot_general(a, b, (((1,), (1,)), ((), ())), preferred_element_type=F32)


def kernel(
    n,
    order_hbm,
    rounds_hbm,
    choice_hbm,
    index_hbm,
    noise_k_hbm,
    noise_v_hbm,
    q_hbm,
    uk_hbm,
    uv_hbm,
    pk_hbm,
    pv_hbm,
    ck_hbm,
    cv_hbm,
    out,
    order_ref,
    rounds_ref,
    choice_ref,
    index_ref,
    table,
    q,
    uk,
    uv,
    own,
    prev,
    col,
    oth,
    com,
    cand,
    pair,
    half,
    maskf,
    local_sem,
    gsend,
    grecv,
    fsend,
    frecv,
    hsend,
    hrecv,
    ssend,
    srecv,
):
    slots, block, _ = own.shape
    width = noise_k_hbm.shape[1]
    heads = width // FEATURE_DIM
    me = lax.axis_index("blk")
    barrier = pltpu.get_barrier_semaphore()

    rows = n // 2
    row, par = me // 2, lax.rem(me, 2)
    partner = me + 1 - 2 * par

    def greet(d):
        pl.semaphore_signal(
            barrier, inc=1, device_id={"blk": lax.rem(me + d, n)}, device_id_type=MESH
        )

    greet(1)
    greet(n - 1)
    pl.loop(1, rows)(lambda d: greet(2 * d))

    loads = [
        pltpu.make_async_copy(src, dst, local_sem.at[i])
        for i, (src, dst) in enumerate(
            (
                (order_hbm, order_ref),
                (rounds_hbm, rounds_ref),
                (choice_hbm, choice_ref),
                (noise_k_hbm, table.at[:, pl.ds(0, width)]),
                (noise_v_hbm, table.at[:, pl.ds(width, width)]),
                (uk_hbm.at[:, 0], uk),
                (uv_hbm.at[:, 0], uv),
                (pk_hbm.at[0, 0], col.at[row, :, pl.ds(0, width)]),
                (pv_hbm.at[0, 0], col.at[row, :, pl.ds(width, width)]),
                (ck_hbm.at[0], cand.at[0]),
                (cv_hbm.at[0], cand.at[1]),
                (index_hbm, index_ref),
                (q_hbm.at[:, 0], q),
            )
        )
    ]
    for load in loads:
        load.start()
    for load in loads[:7]:
        load.wait()

    entries = table.shape[0]
    row_n = lax.broadcasted_iota(jnp.int32, (entries, block), 0)
    row_b = lax.broadcasted_iota(jnp.int32, (block, block), 0)
    col_b = lax.broadcasted_iota(jnp.int32, (block, block), 1)
    ones_n = jnp.ones((entries, FEATURE_DIM), BF16)
    for s in range(slots):
        hidden = order_ref[s] >= UNMASK * rounds_ref[s]
        noise = jnp.where((row_n == choice_ref[s]) & hidden, 1.0, 0.0).astype(BF16)
        keep = jnp.where((row_b == col_b) & jnp.logical_not(hidden), 1.0, 0.0).astype(BF16)
        shown = jnp.concatenate([uk[s], uv[s]], axis=1)
        own[s] = over_rows(
            jnp.concatenate([noise, keep], axis=0), jnp.concatenate([table[...], shown], axis=0)
        ).astype(BF16)
        maskf[s] = over_rows(noise, ones_n)

    for load in loads[7:11]:
        load.wait()
    pl.semaphore_wait(barrier, rows + 1)

    after = lax.rem(me + 1, n)
    wrap = me // (n - 1)

    def shift(s):
        to = lax.rem(s + wrap, slots)
        return pltpu.make_async_remote_copy(
            src_ref=own.at[s],
            dst_ref=prev.at[to],
            send_sem=ssend.at[s],
            recv_sem=srecv.at[to],
            device_id={"blk": after},
            device_id_type=MESH,
        )

    def spread(d):
        return pltpu.make_async_remote_copy(
            src_ref=col.at[row],
            dst_ref=col.at[row],
            send_sem=gsend.at[d],
            recv_sem=grecv.at[row],
            device_id={"blk": 2 * lax.rem(row + d, rows) + par},
            device_id_type=MESH,
        )

    def spread_in(j):
        return pltpu.make_async_remote_copy(
            src_ref=col.at[j],
            dst_ref=col.at[j],
            send_sem=gsend.at[0],
            recv_sem=grecv.at[j],
            device_id={"blk": partner},
            device_id_type=MESH,
        )

    def relay(j):
        return pltpu.make_async_remote_copy(
            src_ref=col.at[j],
            dst_ref=oth.at[j],
            send_sem=fsend.at[j],
            recv_sem=frecv.at[j],
            device_id={"blk": partner},
            device_id_type=MESH,
        )

    def swap(mine):
        return pltpu.make_async_remote_copy(
            src_ref=cand.at[1 - par],
            dst_ref=pair.at[mine],
            send_sem=hsend.at[0],
            recv_sem=hrecv.at[rows],
            device_id={"blk": partner},
            device_id_type=MESH,
        )

    def pick(d):
        return pltpu.make_async_remote_copy(
            src_ref=half.at[row],
            dst_ref=half.at[row],
            send_sem=hsend.at[d],
            recv_sem=hrecv.at[row],
            device_id={"blk": 2 * lax.rem(row + d, rows) + par},
            device_id_type=MESH,
        )

    def pick_in(j):
        return pltpu.make_async_remote_copy(
            src_ref=half.at[j],
            dst_ref=half.at[j],
            send_sem=hsend.at[0],
            recv_sem=hrecv.at[j],
            device_id={"blk": partner},
            device_id_type=MESH,
        )

    def chosen(mine):
        return pltpu.make_async_remote_copy(
            src_ref=com.at[mine],
            dst_ref=com.at[mine],
            send_sem=fsend.at[rows],
            recv_sem=frecv.at[rows],
            device_id={"blk": partner},
            device_id_type=MESH,
        )

    def shift_in(s):
        return pltpu.make_async_remote_copy(
            src_ref=own.at[s],
            dst_ref=prev.at[s],
            send_sem=ssend.at[s],
            recv_sem=srecv.at[s],
            device_id={"blk": after},
            device_id_type=MESH,
        )

    swap(par).start()

    @pl.loop(1, rows)
    def _(d):
        spread(d).start()

    relay(row).start()

    for s in range(slots):
        shift(s).start()

    loads[11].wait()
    owner = index_ref[0]
    pair[par] = cand[par]
    swap(1 - par).wait_recv()
    half[row] = pair[lax.rem(owner, 2)]

    @pl.loop(1, rows)
    def _(d):
        pick(d).start()

    @pl.loop(1, rows)
    def _(d):
        j = lax.rem(row + d, rows)
        spread_in(j).wait_recv()
        relay(j).start()

    @pl.loop(1, rows)
    def _(d):
        pick_in(lax.rem(row + d, rows)).wait_recv()

    com[par] = half[owner // 2]
    chosen(par).start()
    loads[12].wait()

    @pl.loop(0, rows)
    def _(j):
        relay(j).wait_recv()

    chosen(1 - par).wait_recv()

    factor = FEATURE_DIM**-0.5 * math.log2(math.e)

    def lanes(g):
        return slice(g * FEATURE_DIM, (g + 1) * FEATURE_DIM)

    def with_ones(v):
        return jnp.concatenate([v, jnp.ones(v.shape, BF16)], axis=1)

    def shared(c, where):
        near = col[pl.ds(c * HALF, HALF), :, where].reshape(HALF * block, FEATURE_DIM)
        far = oth[pl.ds(c * HALF, HALF), :, where].reshape(HALF * block, FEATURE_DIM)
        return jnp.concatenate([near, far], axis=0)

    @pl.loop(0, slots, unroll=2)
    def _(s):
        shift_in(s).wait_recv()
        for g in range(heads):
            first = g * GROUP
            qs = jnp.concatenate([q[s, :, lanes(first + r)] for r in range(GROUP)], axis=0)
            kc, vc = lanes(g), lanes(heads + g)
            k2 = jnp.concatenate([prev[s, :, kc], own[s, :, kc], com[0, :, lanes(g)]], axis=0)
            v2 = jnp.concatenate([prev[s, :, vc], own[s, :, vc], com[1, :, lanes(g)]], axis=0)
            s1 = over_lanes(qs, shared(0, kc))
            s2 = over_lanes(qs, k2)
            top = jnp.maximum(
                jnp.max(s1, axis=1, keepdims=True), jnp.max(s2, axis=1, keepdims=True)
            )
            p1 = jnp.exp2((s1 - top) * factor).astype(BF16)
            p2 = jnp.exp2((s2 - top) * factor).astype(BF16)
            acc = jnp.dot(p1, with_ones(shared(0, vc)), preferred_element_type=F32)
            acc = acc + jnp.dot(p2, with_ones(v2), preferred_element_type=F32)
            if rows > HALF:

                def more(c, state):
                    top, acc = state
                    s1 = over_lanes(qs, shared(c, kc))
                    new = jnp.maximum(top, jnp.max(s1, axis=1, keepdims=True))
                    p1 = jnp.exp2((s1 - new) * factor).astype(BF16)
                    part = jnp.dot(p1, with_ones(shared(c, vc)), preferred_element_type=F32)
                    return new, acc * jnp.exp2((top - new) * factor) + part

                top, acc = lax.fori_loop(1, rows // HALF, more, (top, acc))
            o = acc[:, :FEATURE_DIM] / acc[:, FEATURE_DIM:]
            mask = maskf[s]
            for r in range(GROUP):
                part = o[r * block : (r + 1) * block] * mask
                out[s, 0, :, lanes(first + r)] = part.astype(BF16)

    @pl.loop(1, rows)
    def _(d):
        spread(d).wait_send()

    @pl.loop(0, rows)
    def _(j):
        relay(j).wait_send()

    chosen(par).wait_send()
    swap(par).wait_send()

    @pl.loop(1, rows)
    def _(d):
        pick(d).wait_send()

    for s in range(slots):
        shift_in(s).wait_send()


def on_device(
    n,
    probe_vectors,
    unsettled_lookups,
    unsettled_payloads,
    uncover_ordering,
    rounds_finished,
    random_entry_choice,
    noise_token_keys,
    noise_token_values,
    prefix_key_cache,
    prefix_value_cache,
    completed_keys,
    completed_values,
    committing_index,
):
    slots, _, block, columns = probe_vectors.shape
    width = noise_token_keys.shape[1]
    anywhere = pl.BlockSpec(memory_space=pl.ANY)
    return pl.pallas_call(
        functools.partial(kernel, n),
        out_shape=pltpu.VMEM(probe_vectors.shape, BF16),
        in_specs=[pl.BlockSpec(memory_space=pltpu.HBM)] * 13,
        out_specs=pl.BlockSpec(memory_space=pltpu.VMEM),
        scratch_shapes=[
            pltpu.VMEM(uncover_ordering.shape, jnp.int32),
            pltpu.SMEM((slots,), jnp.int32),
            pltpu.VMEM(random_entry_choice.shape, jnp.int32),
            pltpu.SMEM((1,), jnp.int32),
            pltpu.VMEM((noise_token_keys.shape[0], 2 * width), BF16),
            pltpu.VMEM((slots, block, columns), BF16),
            pltpu.VMEM((slots, block, width), BF16),
            pltpu.VMEM((slots, block, width), BF16),
            pltpu.VMEM((slots, block, 2 * width), BF16),
            pltpu.VMEM((slots, block, 2 * width), BF16),
            pltpu.VMEM((n // 2, block, 2 * width), BF16),
            pltpu.VMEM((n // 2, block, 2 * width), BF16),
            pltpu.VMEM((2, block, width), BF16),
            pltpu.VMEM((2, block, width), BF16),
            pltpu.VMEM((2, block, width), BF16),
            pltpu.VMEM((n // 2, block, width), BF16),
            pltpu.VMEM((slots, block, FEATURE_DIM), F32),
            pltpu.SemaphoreType.DMA((13,)),
            pltpu.SemaphoreType.DMA((n // 2,)),
            pltpu.SemaphoreType.DMA((n // 2,)),
            pltpu.SemaphoreType.DMA((n // 2 + 1,)),
            pltpu.SemaphoreType.DMA((n // 2 + 1,)),
            pltpu.SemaphoreType.DMA((n // 2,)),
            pltpu.SemaphoreType.DMA((n // 2 + 1,)),
            pltpu.SemaphoreType.DMA((slots,)),
            pltpu.SemaphoreType.DMA((slots,)),
        ],
        compiler_params=pltpu.CompilerParams(
            collective_id=0, has_side_effects=True, vmem_limit_bytes=60 * 2**20
        ),
    )(
        uncover_ordering,
        rounds_finished.reshape(slots),
        random_entry_choice,
        committing_index,
        noise_token_keys,
        noise_token_values,
        probe_vectors,
        unsettled_lookups,
        unsettled_payloads,
        prefix_key_cache,
        prefix_value_cache,
        completed_keys,
        completed_values,
    )


def solution(mesh):
    wide = P("groups", "blk", None, "mp")
    placed = (
        wide,
        wide,
        wide,
        P("groups", "blk", None),
        P("groups", "blk"),
        P("groups", "blk", None),
        P(None, "mp"),
        P(None, "mp"),
        wide,
        wide,
        P(("groups", "blk"), None, "mp"),
        P(("groups", "blk"), None, "mp"),
        P("groups"),
    )
    return jax.shard_map(
        functools.partial(on_device, mesh.shape["blk"]),
        mesh=mesh,
        in_specs=placed,
        out_specs=wide,
        check_vma=False,
    )
```
